32 devices in a mesh: groups: 1, fsdp: 32 (over z, y, x, core).
Axes of the slice: x: 2, y: 2, z: 4, core: 2. Of those that a mesh axis runs over, the one named last changes fastest.
Arguments:
- tokens: bfloat16 [6144, 8192], P(('groups', 'fsdp')), may hold values from -6 to 6
- out_grad: bfloat16 [6144, 512], P(('groups', 'fsdp')), may hold values from -12 to 12
- base_weight: bfloat16 [8192, 512], P('fsdp'), may hold values from -0.0625 to 0.0625
- adapter_ids: int32 [6144], P(('groups', 'fsdp')), may hold values from 0 to 31, as said below
- adapter_home: int32 [32], P('groups'), may hold values from 0 to 31, each once
- factors: float32 [32, 16, 8704], P(('groups', 'fsdp')), may hold values from -6 to 6
- first_moment: float32 [32, 16, 8704], P(('groups', 'fsdp'))
- second_moment: float32 [32, 16, 8704], P(('groups', 'fsdp'))
Outputs:
- value_output: bfloat16 [6144, 512], P(('groups', 'fsdp'))
- input_gradient: bfloat16 [6144, 8192], P(('groups', 'fsdp'))
- new_factors: float32 [32, 16, 8704], P(('groups', 'fsdp'))
- new_first: float32 [32, 16, 8704], P(('groups', 'fsdp'))
- new_second: float32 [32, 16, 8704], P(('groups', 'fsdp'))
The draws below stay inside these ranges and needn't reach their ends.
Inputs may be any that keep to these rules, and one draw needn't show every extreme that they name: `adapter_ids`: on each device every adapter has between 0 and 12 tokens; one adapter, the same on all devices, has exactly 12 tokens on every device; on each device the adapters fall into pairs whose counts sum to 12. Adapter k's factors and moments are held on the device whose fsdp index is adapter_home[k]; every index appears once.
All inputs are finite; a program needn't handle non-finite values.
Results may differ from the reference program's by a relative error of at most 0.0062.
Values may be sent and summed in bfloat16 or wider, within the bound.
No kernel may reach another device: no remote copies, remote signals or barrier semaphores. Data moves between devices by JAX's collectives and lax.ppermute only.
A program may use at most 128 MiB of HBM per device.

```python
import math
import jax
import jax.numpy as jnp
from jax import lax

D = 8192
KV = 512
R = 16
TOK_DEV = 192
ADAPTERS = 32
TOKENS = 6144


def draw_adapter_ids(key, part):
    key = jax.random.fold_in(key, 7)
    devices = TOKENS // TOK_DEV
    half_count = ADAPTERS // 2
    mean_count = TOK_DEV // ADAPTERS
    busy_key, rest_key = jax.random.split(key)
    busiest = jax.random.randint(busy_key, (), 0, ADAPTERS)

    def one_device(device_key):
        order_key, spread_key, place_key = jax.random.split(device_key, 3)
        ranking = jax.random.permutation(order_key, ADAPTERS).astype(jnp.int32)
        leading = ranking[0]
        ranking = jnp.where(ranking == busiest, leading, ranking)
        ranking = ranking.at[0].set(busiest)
        spread = jax.random.randint(spread_key, (half_count,), 0, mean_count + 1)
        spread = spread.at[0].set(mean_count)
        amounts = jnp.concatenate([mean_count + spread, mean_count - spread]).astype(jnp.int32)
        counts = jnp.zeros((ADAPTERS,), jnp.int32).at[ranking].set(amounts)
        labels = jnp.repeat(jnp.arange(ADAPTERS, dtype=jnp.int32), counts, total_repeat_length=TOK_DEV)
        return labels[jax.random.permutation(place_key, TOK_DEV)]
    device_keys = jax.random.split(rest_key, devices)
    return jax.vmap(one_device)(device_keys).reshape(TOKENS).astype(jnp.int32)


def earlier_gradients(key, power):
    shape = (ADAPTERS, R, D + KV)
    column = jnp.arange(D + KV)
    down_scale = 0.5 * math.sqrt(KV * TOK_DEV / D)
    up_scale = 0.5 * math.sqrt(TOK_DEV)
    scale = jnp.where(column < D, down_scale, up_scale).astype(jnp.float32)
    older_key, latest_key = jax.random.split(key, 2)
    lower = 0.3 ** power
    upper = 3.0 ** power

    def one_gradient(grad_key):
        sign_key, size_key = jax.random.split(grad_key)
        signs = jax.random.rademacher(sign_key, shape, jnp.float32)
        spread = jax.random.uniform(size_key, shape, jnp.float32)
        sizes = (lower + spread * (upper - lower)) ** (1.0 / power)
        return signs * sizes
    older = one_gradient(older_key) * scale
    latest = one_gradient(latest_key) * scale
    return (older, latest)


def draw_first_moment(key, part):
    older, latest = earlier_gradients(key, 0.1)
    return (0.1 * (0.9 * older + latest)).astype(jnp.float32)


def draw_second_moment(key, part):
    older, latest = earlier_gradients(key, 0.1)
    return (0.05 * (0.95 * older * older + latest * latest)).astype(jnp.float32)


def levels(rng, shape, cuts, smallest, top_value):
    def one(position, shards_of):
        heights = jax.random.uniform(jax.random.fold_in(jax.random.fold_in(rng, 6), position), (shards_of,), jnp.float32, smallest / len(cuts), top_value / len(cuts))
        return jnp.repeat(jnp.exp(heights), shape[position] // shards_of).reshape((-1,) + (1,) * (len(shape) - position - 1))

    level = one(*cuts[0])
    for cut in cuts[1:]:
        level = level * one(*cut)
    return level


def noise(rng, extent, scale, reach, pieces=(), kind=jnp.bfloat16):
    loudness = levels(rng, extent, pieces, -0.22, 0.18) if pieces else 1.0
    array = jax.random.normal(rng, extent, jnp.float32) * scale * loudness
    return jnp.minimum(jnp.maximum(array, -reach), reach).astype(kind)


def setup_inputs(seed: int = 0, part: int = 0) -> dict:
    key_list = jax.random.split(jax.random.key(seed), 9)
    own_keys = jax.random.split(jax.random.fold_in(key_list[8], part), 9)
    return {
        "tokens": noise(own_keys[0], (TOKENS, D), 1.0, 6.0, ((0, 32),)),
        "out_grad": noise(own_keys[1], (TOKENS, KV), 2.0, 12.0, ((0, 32),)),
        "base_weight": noise(key_list[2], (D, KV), D ** -0.5, 0.0625, ((0, 32),)),
        "adapter_ids": draw_adapter_ids(jax.random.fold_in(jax.random.fold_in(key_list[8], part), 71), part),
        "adapter_home": jax.random.permutation(own_keys[4], ADAPTERS).astype(jnp.int32),
        "factors": noise(own_keys[5], (ADAPTERS, R, D + KV), 1.0, 6.0, ((0, 32),), jnp.float32),
        "first_moment": draw_first_moment(jax.random.fold_in(jax.random.fold_in(key_list[8], part), 71), part),
        "second_moment": draw_second_moment(jax.random.fold_in(jax.random.fold_in(key_list[8], part), 71), part),
    }


adapter_scale = 0.25
beta_first = 0.9
beta_second = 0.95
adam_eps = 1e-08
learn_rate = 0.05
bias_first = 0.271
bias_second = 0.142625

def reference(tokens, out_grad, base_weight, adapter_ids, adapter_home, factors, first_moment, second_moment):
    total_tokens, feature_width = tokens.shape
    value_width = out_grad.shape[1]
    adapter_count = factors.shape[0]
    input_scale = 1.0 / math.sqrt(feature_width)
    compute = factors.astype(jnp.bfloat16)
    down_projection_matrix = compute[:, :, :feature_width]
    up_projection_matrix = compute[:, :, feature_width:]
    state_rows = adapter_home[adapter_ids].astype(jnp.int32)
    block_rows = min(256, total_tokens)
    block_count = total_tokens // block_rows

    def one_block(totals, block_index):
        offset = (block_index * block_rows).astype(jnp.int32)
        token_block = lax.dynamic_slice_in_dim(tokens, offset, block_rows, 0)
        grad_block = lax.dynamic_slice_in_dim(out_grad, offset, block_rows, 0)
        row_block = lax.dynamic_slice_in_dim(state_rows, offset, block_rows, 0)
        down_projection_rows = down_projection_matrix[row_block].astype(jnp.float32)
        up_projection_rows = up_projection_matrix[row_block].astype(jnp.float32)
        token_wide = token_block.astype(jnp.float32)
        wide_gradient = grad_block.astype(jnp.float32)
        projected_rows = (input_scale * jnp.einsum('td,trd->tr', token_wide, down_projection_rows)).astype(jnp.bfloat16)
        adapter_value = (adapter_scale * jnp.einsum('wn,wnd->wd', projected_rows.astype(jnp.float32), up_projection_rows)).astype(jnp.bfloat16)
        narrow_gradient = (adapter_scale * jnp.einsum('fz,fgz->fg', wide_gradient, up_projection_rows)).astype(jnp.bfloat16)
        adapter_input = (input_scale * jnp.einsum('gv,gvl->gl', narrow_gradient.astype(jnp.float32), down_projection_rows)).astype(jnp.bfloat16)
        frozen_value_rows = jnp.dot(token_block, base_weight, preferred_element_type=jnp.float32)
        frozen_input_rows = jnp.dot(grad_block, base_weight.T, preferred_element_type=jnp.float32)
        value_output = (frozen_value_rows + adapter_value.astype(jnp.float32)).astype(jnp.bfloat16)
        input_gradient = (frozen_input_rows + adapter_input.astype(jnp.float32)).astype(jnp.bfloat16)
        down_terms = input_scale * narrow_gradient.astype(jnp.float32)[:, :, None] * token_wide[:, None, :]
        up_projection_terms = adapter_scale * projected_rows.astype(jnp.float32)[:, :, None] * wide_gradient[:, None, :]
        grad_terms = jnp.concatenate([down_terms, up_projection_terms], axis=2)
        totals = totals + jax.ops.segment_sum(grad_terms, row_block, num_segments=adapter_count)
        return (totals, (value_output, input_gradient))
    start_totals = jnp.zeros(factors.shape, jnp.float32)
    gradient_list, (value_blocks, input_blocks) = lax.scan(one_block, start_totals, jnp.arange(block_count, dtype=jnp.int32))
    value_output = value_blocks.reshape(total_tokens, value_width)
    input_gradient = input_blocks.reshape(total_tokens, feature_width)
    new_first = beta_first * first_moment + (1.0 - beta_first) * gradient_list
    new_second = beta_second * second_moment + (1.0 - beta_second) * gradient_list * gradient_list
    adam_step = new_first / bias_first / (jnp.sqrt(new_second / bias_second) + adam_eps)
    new_factors = factors - learn_rate * adam_step
    return (value_output, input_gradient, new_factors, new_first, new_second)
```

```python
import math

import jax
import jax.numpy as jnp
from jax import lax
from jax.sharding import PartitionSpec as P

adapter_scale = 0.25
beta_first = 0.9
beta_second = 0.95
adam_eps = 1e-08
learn_rate = 0.05
bias_first = 0.271
bias_second = 0.142625
contract_last = (((1,), (1,)), ((), ()))
contract_first = (((0,), (0,)), ((), ()))


def local(
    tokens, out_grad, base_weight, adapter_ids, adapter_home, factors, first_moment, second_moment
):
    tok_count, feature_width = tokens.shape
    devices = lax.axis_size("fsdp")
    rank = factors.shape[1]
    input_scale = 1.0 / math.sqrt(feature_width)
    compute = factors[0].astype(jnp.bfloat16)
    up_all = lax.all_gather(compute[:, feature_width:], "fsdp", axis=0, tiled=True)
    down_all = lax.all_gather(compute[:, :feature_width], "fsdp", axis=0, tiled=True)
    weight = lax.all_gather(base_weight, "fsdp", axis=0, tiled=True)

    columns = jnp.arange(devices, dtype=jnp.int32)
    adapter_hot = (adapter_ids[:, None] == columns[None, :]).astype(jnp.int32)
    target = jnp.sum(adapter_hot * adapter_home[None, :], axis=1)
    mask = target[:, None] == jnp.arange(devices * rank, dtype=jnp.int32)[None, :] // rank

    def masked(x):
        return jnp.where(mask, x, 0.0).astype(jnp.bfloat16)

    low_grad = masked(
        adapter_scale
        * lax.dot_general(out_grad, up_all, contract_last, preferred_element_type=jnp.float32)
    )
    down_grad = (
        input_scale
        * lax.dot_general(low_grad, tokens, contract_first, preferred_element_type=jnp.float32)
    ).astype(jnp.bfloat16)
    down_sum = lax.psum_scatter(down_grad, "fsdp", scatter_dimension=0, tiled=True)
    projected = masked(
        input_scale
        * lax.dot_general(tokens, down_all, contract_last, preferred_element_type=jnp.float32)
    )
    up_grad = adapter_scale * lax.dot_general(
        projected, out_grad, contract_first, preferred_element_type=jnp.float32
    )
    up_sum = lax.psum_scatter(up_grad, "fsdp", scatter_dimension=0, tiled=True)
    own_values = (
        adapter_scale * jnp.dot(projected, up_all, preferred_element_type=jnp.float32)
    ).astype(jnp.bfloat16)
    own_inputs = (
        input_scale * jnp.dot(low_grad, down_all, preferred_element_type=jnp.float32)
    ).astype(jnp.bfloat16)
    frozen_value_rows = jnp.dot(tokens, weight, preferred_element_type=jnp.float32)
    frozen_input_rows = lax.dot_general(
        out_grad, weight, contract_last, preferred_element_type=jnp.float32
    )
    value_output = (frozen_value_rows + own_values.astype(jnp.float32)).astype(jnp.bfloat16)
    input_gradient = (frozen_input_rows + own_inputs.astype(jnp.float32)).astype(jnp.bfloat16)
    gradient_list = jnp.concatenate([down_sum.astype(jnp.float32), up_sum], axis=1)[None]
    new_first = beta_first * first_moment + (1.0 - beta_first) * gradient_list
    new_second = beta_second * second_moment + (1.0 - beta_second) * gradient_list * gradient_list
    adam_step = new_first / bias_first / (jnp.sqrt(new_second / bias_second) + adam_eps)
    new_factors = factors - learn_rate * adam_step
    return (value_output, input_gradient, new_factors, new_first, new_second)


def solution(mesh):
    placed = (
        P(("groups", "fsdp"), None),
        P(("groups", "fsdp"), None),
        P("fsdp", None),
        P(("groups", "fsdp")),
        P("groups"),
        P(("groups", "fsdp"), None, None),
        P(("groups", "fsdp"), None, None),
        P(("groups", "fsdp"), None, None),
    )
    return jax.shard_map(
        local,
        mesh=mesh,
        in_specs=placed,
        out_specs=(
            P(("groups", "fsdp"), None),
            P(("groups", "fsdp"), None),
            P(("groups", "fsdp"), None, None),
            P(("groups", "fsdp"), None, None),
            P(("groups", "fsdp"), None, None),
        ),
        check_vma=False,
    )
```

```python
import functools
import math

import jax
import jax.numpy as jnp
from jax import lax
from jax.experimental import pallas as pl
from jax.experimental.pallas import tpu as pltpu
from jax.sharding import PartitionSpec as P

adapter_scale = 0.25
beta_first = 0.9
beta_second = 0.95
adam_eps = 1e-08
learn_rate = 0.05
bias_first = 0.271
bias_second = 0.142625
contract_last = (((1,), (1,)), ((), ()))
contract_first = (((0,), (0,)), ((), ()))
f32 = jnp.float32
bf16 = jnp.bfloat16
vmem_bytes = 48 * 2**20


def dot(a, b, dims=(((1,), (0,)), ((), ()))):
    return lax.dot_general(a, b, dims, preferred_element_type=f32)


class Plan:
    def __init__(self, devices):
        self.devices = devices
        self.chips = devices // 2
        bits = self.chips.bit_length() - 1
        self.basis = (1, 2, 4, 12) if self.chips == 16 else tuple(1 << i for i in range(bits))
        self.bits = bits

    def order(self, stream, core):
        turn = (self.bits // 2 if stream == "d" else 0) + core
        return tuple(self.basis[(i + turn) % self.bits] for i in range(self.bits))

    def masks(self, stream, core):
        order = self.order(stream, core)
        out = []
        for b in range(self.chips):
            m = 0
            for i, flip in enumerate(order):
                if b >> i & 1:
                    m ^= flip
            out.append(m)
        return out

    def by_core(self, core, stream):
        return jnp.where(
            core == 0,
            jnp.array(self.masks(stream, 0), jnp.int32),
            jnp.array(self.masks(stream, 1), jnp.int32),
        )

    def swap(self, x):
        return lax.ppermute(x, "fsdp", [(i, i ^ 1) for i in range(self.devices)])

    def step(self, x, stream, i):
        pairs = []
        for d in range(self.devices):
            flip = self.order(stream, d & 1)[i]
            pairs.append((d, ((d >> 1) ^ flip) << 1 | (d & 1)))
        return lax.ppermute(x, "fsdp", pairs)


whole_vmem = pl.BlockSpec(memory_space=pltpu.VMEM)
anywhere = pl.BlockSpec(memory_space=pl.ANY)


def params():
    return pltpu.CompilerParams(vmem_limit_bytes=vmem_bytes)


def join_kernel(count, *refs):
    for i in range(count):
        own, got, out = refs[2 * i], refs[2 * i + 1], refs[2 * count + i]
        rows = own.shape[0]
        out[:rows] = own[...]
        out[rows:] = got[...]


def join(pairs):
    count = len(pairs)
    flat = [x for pair in pairs for x in pair]
    return pl.pallas_call(
        functools.partial(join_kernel, count),
        in_specs=[whole_vmem] * (2 * count),
        out_specs=[whole_vmem] * count,
        out_shape=[jax.ShapeDtypeStruct((2 * x.shape[0], x.shape[1]), x.dtype) for x, _ in pairs],
        compiler_params=params(),
        cost_estimate=pl.CostEstimate(
            flops=0, bytes_accessed=4 * sum(x.size for x in flat), transcendentals=0
        ),
    )(*flat)


def fold_kernel(count, *refs):
    for i in range(count):
        keep, got = refs[2 * i], refs[2 * i + 1]
        kept, sent = refs[2 * count + 2 * i], refs[2 * count + 2 * i + 1]
        half = kept.shape[0]
        kept[...] = (keep[:half].astype(f32) + got[:half].astype(f32)).astype(kept.dtype)
        sent[...] = (keep[half:].astype(f32) + got[half:].astype(f32)).astype(sent.dtype)


def fold(pairs):
    count = len(pairs)
    flat = [x for pair in pairs for x in pair]
    shapes = [
        jax.ShapeDtypeStruct((x.shape[0] // 2, x.shape[1]), x.dtype) for x, _ in pairs for _ in "ks"
    ]
    out = pl.pallas_call(
        functools.partial(fold_kernel, count),
        in_specs=[whole_vmem] * (2 * count),
        out_specs=[whole_vmem] * (2 * count),
        out_shape=shapes,
        compiler_params=params(),
        cost_estimate=pl.CostEstimate(
            flops=sum(x.size for x in flat),
            bytes_accessed=4 * sum(x.size for x in flat),
            transcendentals=0,
        ),
    )(*flat)
    return [(out[2 * i], out[2 * i + 1]) for i in range(count)]


def tie_kernel(*refs):
    del refs


def tie(arrays, after):
    count = len(arrays)
    return pl.pallas_call(
        tie_kernel,
        in_specs=[anywhere] * (count + len(after)),
        out_specs=[anywhere] * count,
        out_shape=[jax.ShapeDtypeStruct(x.shape, x.dtype) for x in arrays],
        input_output_aliases={i: i for i in range(count)},
        cost_estimate=pl.CostEstimate(flops=0, bytes_accessed=0, transcendentals=0),
    )(*arrays, *after)


def factor_kernel(width, wide, info, f_ref, own_ref, send_ref):
    core = info[0]
    blocks = wide // width
    for i in range(blocks // 2):
        mine = pl.multiple_of((2 * i + core) * width, width)
        other = pl.multiple_of((2 * i + 1 - core) * width, width)
        own_ref[:, i * width : (i + 1) * width] = f_ref[:, pl.ds(mine, width)].astype(bf16)
        send_ref[:, i * width : (i + 1) * width] = f_ref[:, pl.ds(other, width)].astype(bf16)
    up = f_ref[:, wide:].astype(bf16)
    own_ref[:, wide // 2 :] = up
    send_ref[:, wide // 2 :] = up


def split_factors(info, factors, width, wide):
    rank, total = factors.shape
    shape = jax.ShapeDtypeStruct((rank, wide // 2 + total - wide), bf16)
    return pl.pallas_call(
        functools.partial(factor_kernel, width, wide),
        in_specs=[pl.BlockSpec(memory_space=pltpu.SMEM), pl.BlockSpec(memory_space=pltpu.VMEM)],
        out_specs=[pl.BlockSpec(memory_space=pltpu.VMEM)] * 2,
        out_shape=[shape, shape],
        cost_estimate=pl.CostEstimate(flops=0, bytes_accessed=1_000_000, transcendentals=0),
    )(info, factors)


def join_factors_kernel(half, own_ref, got_ref, up_ref, down_ref):
    rank = own_ref.shape[0]
    for at, ref in ((0, own_ref), (rank, got_ref)):
        down_ref[at : at + rank] = ref[:, :half]
        up_ref[at : at + rank] = ref[:, half:]


def join_factors(own, got, half):
    rank, total = own.shape
    return pl.pallas_call(
        functools.partial(join_factors_kernel, half),
        in_specs=[whole_vmem] * 2,
        out_specs=[whole_vmem] * 2,
        out_shape=[
            jax.ShapeDtypeStruct((2 * rank, total - half), bf16),
            jax.ShapeDtypeStruct((2 * rank, half), bf16),
        ],
        cost_estimate=pl.CostEstimate(flops=0, bytes_accessed=8 * rank * total, transcendentals=0),
    )(own, got)


def halves_kernel(width, info, x_ref, own_ref, other_ref):
    core = info[0]
    for i in range(own_ref.shape[1] // width):
        mine = pl.multiple_of((2 * i + core) * width, width)
        other = pl.multiple_of((2 * i + 1 - core) * width, width)
        at = slice(i * width, (i + 1) * width)
        own_ref[:, at] = x_ref[:, pl.ds(mine, width)]
        other_ref[:, at] = x_ref[:, pl.ds(other, width)]


def halves(info, x, width):
    rows, wide = x.shape
    step = rows // 4
    small = pl.BlockSpec((step, wide // 2), lambda i, s: (i, 0))
    return pl.pallas_call(
        functools.partial(halves_kernel, width),
        grid_spec=pltpu.PrefetchScalarGridSpec(
            num_scalar_prefetch=1,
            grid=(4,),
            in_specs=[pl.BlockSpec((step, wide), lambda i, s: (i, 0))],
            out_specs=[small, small],
        ),
        out_shape=[jax.ShapeDtypeStruct((rows, wide // 2), bf16)] * 2,
        cost_estimate=pl.CostEstimate(flops=0, bytes_accessed=rows * wide * 4, transcendentals=0),
    )(info, x)


def down_grad_kernel(half, scale, low_ref, low_two_ref, x_ref, y_ref, ka, sa, kb, sb):
    q = pl.program_id(0)
    n = x_ref.shape[0]

    def one(low, keep, send):
        out = dot(low[:, :n], x_ref[...]) + dot(low[:, n:], y_ref[...])
        out = (scale * out).astype(bf16)
        cut = out.shape[0] // 2
        keep[...] = out[:cut]
        send[...] = out[cut:]

    @pl.when(q < half)
    def _():
        one(low_ref, ka, sa)

    @pl.when(q >= half)
    def _():
        one(low_two_ref, kb, sb)


def down_grads(low, low_two, own, sibling, scale):
    rows, cols = sibling.shape
    blocks = 8
    width = cols // blocks
    half = blocks // 2
    n = low.shape[0]
    whole = pl.BlockSpec(low.shape, lambda q: (0, 0))
    part = pl.BlockSpec((rows, width), lambda q: (0, q))
    first = pl.BlockSpec((n // 2, width), lambda q: (0, jnp.minimum(q, half - 1)))
    second = pl.BlockSpec((n // 2, width), lambda q: (0, jnp.maximum(q - half, 0)))
    out = jax.ShapeDtypeStruct((n // 2, cols // 2), bf16)
    return pl.pallas_call(
        functools.partial(down_grad_kernel, half, scale),
        grid=(blocks,),
        in_specs=[whole, whole, part, part],
        out_specs=[first, first, second, second],
        out_shape=[out] * 4,
        compiler_params=params(),
        cost_estimate=pl.CostEstimate(
            flops=4 * rows * cols * n, bytes_accessed=4 * rows * cols + 2 * n * cols, transcendentals=0
        ),
    )(low, low_two, own, sibling)


def project_kernel(rank, x_ref, y_ref, a_ref, owner_ref, target_ref, add_ref, o_ref, acc):
    q = pl.program_id(0)

    @pl.when(q == 0)
    def _():
        acc[...] = jnp.zeros_like(acc)

    n = x_ref.shape[0]
    acc[:n] += dot(x_ref[...], a_ref[...], contract_last)
    acc[n:] += dot(y_ref[...], a_ref[...], contract_last)

    @pl.when(q == pl.num_programs(0) - 1)
    def _():
        kept = jnp.where(target_ref[...] == owner_ref[...], acc[...], 0.0)
        out = kept[:, :128]
        for i in range(1, kept.shape[1] // 128):
            out = out + kept[:, i * 128 : (i + 1) * 128]
        turn = rank
        while turn < 128:
            out = out + pltpu.roll(out, turn, 1)
            turn *= 2
        o_ref[...] = add_ref[...] + out


def project(own, sibling, down, owner, targets, add, rank):
    rows, cols = sibling.shape
    n = down.shape[0]
    width = cols // 4
    part = pl.BlockSpec((rows, width), lambda q: (0, q))
    still = lambda q: (0, 0)
    return pl.pallas_call(
        functools.partial(project_kernel, rank),
        grid=(4,),
        in_specs=[
            part,
            part,
            pl.BlockSpec((n, width), lambda q: (0, q)),
            pl.BlockSpec((1, n), still),
            pl.BlockSpec((2 * rows, 1), still),
            pl.BlockSpec((2 * rows, 128), still),
        ],
        out_specs=pl.BlockSpec((2 * rows, 128), still),
        out_shape=jax.ShapeDtypeStruct((2 * rows, 128), f32),
        scratch_shapes=[pltpu.VMEM((2 * rows, n), f32)],
        compiler_params=params(),
        cost_estimate=pl.CostEstimate(
            flops=4 * rows * cols * n, bytes_accessed=(4 * rows + 2 * n) * cols, transcendentals=0
        ),
    )(own, sibling, down, owner, targets, add)


def frozen_kernel(half, width, scale, info, *refs):
    x0, x1, y0, y1, a0, a1, b0, b1, u_ref, w_ref, g_ref, low_ref, v_ref, o_ref, t_ref = refs
    b = pl.program_id(0)

    @pl.when(b == 0)
    def _():
        v_ref[...] = jnp.zeros_like(v_ref)

    n = x0.shape[0]
    cut = a0.shape[0]
    v_ref[:n] += dot(x0[...], u_ref[...]) + dot(x1[...], w_ref[...])
    v_ref[n:] += dot(y0[...], u_ref[...]) + dot(y1[...], w_ref[...])
    for part, one, two, rows in ((0, a0, b0, u_ref), (half, a1, b1, w_ref)):
        lora = scale * (dot(low_ref[:, :cut], one[...]) + dot(low_ref[:, cut:], two[...]))
        out = dot(g_ref[...], rows[...], contract_last) + lora.astype(bf16).astype(f32)
        out = out.astype(bf16)
        at = pl.ds(pl.multiple_of(info[1 + part + b] * width, width), width)
        o_ref[:, at] = out[:n]
        t_ref[:, at] = out[n:]


def frozen(info, own, sibling, grads, low, down_a, down_b, weight_a, weight_b, width, scale):
    rows, cols = sibling.shape
    half = cols // width // 2
    n = down_a.shape[0]
    kv = grads.shape[1]
    still = lambda b, s: (0, 0)
    early = lambda b, s: (0, s[1 + b])
    late = lambda b, s: (0, s[1 + half + b])
    return pl.pallas_call(
        functools.partial(frozen_kernel, half, width, scale),
        grid_spec=pltpu.PrefetchScalarGridSpec(
            num_scalar_prefetch=1,
            grid=(half,),
            in_specs=[pl.BlockSpec((rows, width), early), pl.BlockSpec((rows, width), late)] * 2
            + [pl.BlockSpec((n, width), early), pl.BlockSpec((n, width), late)] * 2
            + [pl.BlockSpec((width, kv), lambda b, s: (b, 0))] * 2
            + [pl.BlockSpec((2 * rows, kv), still), pl.BlockSpec((2 * rows, 2 * n), still)],
            out_specs=[
                pl.BlockSpec((2 * rows, kv), still),
                pl.BlockSpec((rows, cols), still),
                pl.BlockSpec((rows, cols), still),
            ],
        ),
        out_shape=[
            jax.ShapeDtypeStruct((2 * rows, kv), f32),
            jax.ShapeDtypeStruct((rows, cols), bf16),
            jax.ShapeDtypeStruct((rows, cols), bf16),
        ],
        compiler_params=params(),
        cost_estimate=pl.CostEstimate(
            flops=8 * rows * cols * (n + kv),
            bytes_accessed=(8 * rows + 4 * n + 2 * kv) * cols,
            transcendentals=0,
        ),
    )(info, own, own, sibling, sibling, down_a, down_a, down_b, down_b, weight_a, weight_b, grads, low)


def merge_kernel(width, info, own_ref, got_ref, o_ref):
    core = info[0]
    for i in range(own_ref.shape[1] // width):
        mine = pl.multiple_of((2 * i + core) * width, width)
        other = pl.multiple_of((2 * i + 1 - core) * width, width)
        at = slice(i * width, (i + 1) * width)
        o_ref[:, pl.ds(mine, width)] = own_ref[:, at]
        o_ref[:, pl.ds(other, width)] = got_ref[:, at]


def merge(info, own, got, width):
    rows, cols = own.shape
    step = rows // 4
    small = pl.BlockSpec((step, cols), lambda i, s: (i, 0))
    return pl.pallas_call(
        functools.partial(merge_kernel, width),
        grid_spec=pltpu.PrefetchScalarGridSpec(
            num_scalar_prefetch=1,
            grid=(4,),
            in_specs=[small, small],
            out_specs=pl.BlockSpec((step, 2 * cols), lambda i, s: (i, 0)),
        ),
        out_shape=jax.ShapeDtypeStruct((rows, 2 * cols), own.dtype),
        cost_estimate=pl.CostEstimate(flops=0, bytes_accessed=8 * rows * cols, transcendentals=0),
    )(info, own, got)


def adam_kernel(width, info, f_ref, m_ref, v_ref, own_ref, got_ref, nf_ref, nm_ref, nv_ref):
    core = info[0]
    for i in range(f_ref.shape[1] // (2 * width)):
        own = own_ref[:, i * width : (i + 1) * width]
        got = got_ref[:, i * width : (i + 1) * width]
        left = jnp.where(core == 0, own, got)
        right = jnp.where(core == 0, got, own)
        for k, g in ((2 * i, left), (2 * i + 1, right)):
            at = slice(k * width, (k + 1) * width)
            first = beta_first * m_ref[:, at] + (1.0 - beta_first) * g
            second = beta_second * v_ref[:, at] + (1.0 - beta_second) * g * g
            step = first / bias_first / (jnp.sqrt(second / bias_second) + adam_eps)
            nf_ref[:, at] = f_ref[:, at] - learn_rate * step
            nm_ref[:, at] = first
            nv_ref[:, at] = second


def adam(info, factors, first, second, own, got, width):
    shape = jax.ShapeDtypeStruct(factors.shape, f32)
    vmem = pl.BlockSpec(memory_space=pltpu.VMEM)
    return pl.pallas_call(
        functools.partial(adam_kernel, width),
        in_specs=[pl.BlockSpec(memory_space=pltpu.SMEM)] + [vmem] * 5,
        out_specs=[vmem] * 3,
        out_shape=[shape] * 3,
        compiler_params=pltpu.CompilerParams(vmem_limit_bytes=vmem_bytes),
        cost_estimate=pl.CostEstimate(
            flops=20 * factors.size, bytes_accessed=32 * factors.size, transcendentals=0
        ),
    )(info, factors, first, second, own, got)


def local(
    tokens, out_grad, base_weight, adapter_ids, adapter_home, factors, first_moment, second_moment
):
    tok_count, feature_width = tokens.shape
    value_width = out_grad.shape[1]
    rank = factors.shape[1]
    width = base_weight.shape[0]
    plan = Plan(lax.axis_size("fsdp"))
    devices, chips = plan.devices, plan.chips
    half = feature_width // 2
    input_scale = 1.0 / math.sqrt(feature_width)
    me = lax.axis_index("fsdp")
    chip, core = me >> 1, me & 1
    mask_d = plan.by_core(core, "d")
    mask_w = plan.by_core(core, "w")
    info = jnp.concatenate([core[None].astype(jnp.int32), (chip ^ mask_w).astype(jnp.int32)])
    bits = plan.bits

    own_factors, sent_factors = split_factors(info, factors[0], width, feature_width)
    weight = base_weight
    got_weight = plan.step(weight, "w", 0)
    got_factors = plan.swap(sent_factors)
    up, down = join_factors(own_factors, got_factors, half)

    columns = jnp.arange(devices, dtype=jnp.int32)
    adapter_hot = (adapter_ids[:, None] == columns[None, :]).astype(jnp.int32)
    target = jnp.sum(adapter_hot * adapter_home[None, :], axis=1)
    tail = jnp.broadcast_to(target[:, None], (tok_count, 128)).astype(bf16)
    mine = jnp.concatenate([out_grad, tail], axis=1)
    theirs = plan.swap(mine)
    own_half, sent_half = halves(info, tokens, width)
    sibling = plan.swap(sent_half)
    both = jnp.concatenate([mine, theirs], axis=0)
    grads = both[:, :value_width]
    targets = both[:, value_width : value_width + 1].astype(jnp.int32)

    for i in range(bits - 1):
        if i > 0:
            got_weight = plan.step(weight, "w", i)
        got_down = plan.step(down, "d", i)
        got_up = plan.step(up, "d", i)
        weight, down, up = join(((weight, got_weight), (down, got_down), (up, got_up)))
    up_all = jnp.concatenate([up, plan.step(up, "d", bits - 1)], axis=0)
    weight_a, weight_b = weight, plan.step(weight, "w", bits - 1)
    down_a, down_b = down, plan.step(down, "d", bits - 1)

    within = jnp.arange(2 * rank, dtype=jnp.int32) // rank
    cores = jnp.where(within == 0, core, 1 - core)

    def owner_of(mask):
        return (2 * (chip ^ mask)[:, None] + cores[None, :]).reshape(1, -1).astype(jnp.int32)

    owner = owner_of(mask_d)
    owner_two = owner_of(mask_w)
    keep = targets == owner
    places = [[plan.masks("d", c).index(m) for m in plan.masks("w", c)] for c in (0, 1)]
    where = jnp.where(core == 0, jnp.array(places[0], jnp.int32), jnp.array(places[1], jnp.int32))
    up_two = up_all.reshape(chips, 2 * rank, value_width)[where].reshape(up_all.shape)

    def low_of(up, owner):
        out = adapter_scale * dot(up, grads, contract_last)
        return jnp.where(owner.reshape(-1, 1) == targets.reshape(1, -1), out, 0.0).astype(bf16)

    low = jnp.where(keep, adapter_scale * dot(grads, up_all, contract_last), 0.0).astype(bf16)
    keep_a, send_a, keep_b, send_b = down_grads(
        low_of(up_all, owner), low_of(up_two, owner_two), own_half, sibling, input_scale
    )
    n = down_a.shape[0]
    nothing = jnp.zeros((2 * tok_count, 128), f32)
    part_a = project(own_half, sibling, down_a, owner[:, :n], targets, nothing, rank)

    send_a, send_b = tie((send_a, send_b), (weight_b, down_b))
    for i in reversed(range(bits)):
        got_a = plan.step(send_a, "d", i)
        got_b = plan.step(send_b, "w", i)
        if i > 0:
            (keep_a, send_a), (keep_b, send_b) = fold(((keep_a, got_a), (keep_b, got_b)))
    sum_a = keep_a.astype(f32) + got_a.astype(f32)
    sum_b = keep_b.astype(f32) + got_b.astype(f32)

    part = project(own_half, sibling, down_b, owner[:, n:], targets, part_a, rank)
    other = plan.swap(part)
    total = part + jnp.concatenate([other[tok_count:], other[:tok_count]], axis=0)
    repeated = jnp.tile((input_scale * total).astype(bf16), (1, keep.shape[1] // 128))
    projected = jnp.where(keep, repeated, jnp.zeros((), bf16))
    own_blocks = [
        jnp.where(
            core == 0,
            grads[:, 2 * i * width : (2 * i + 1) * width],
            grads[:, (2 * i + 1) * width : (2 * i + 2) * width],
        )
        for i in range(value_width // (2 * width))
    ]
    half_grads = jnp.concatenate(own_blocks, axis=1)
    up_grad = adapter_scale * dot(projected, half_grads, contract_first)
    cut = up_grad.shape[0] // 2
    keep_up, send_up = up_grad[:cut], up_grad[cut:]
    for i in reversed(range(bits)):
        got_up = plan.step(send_up, "d", i)
        cut = cut // 2
        if i > 0:
            send_up = keep_up[cut:] + got_up[cut:]
            keep_up = keep_up[:cut] + got_up[:cut]
    sum_up = keep_up + got_up
    own_values = (adapter_scale * dot(projected[:tok_count], up_all)).astype(bf16)

    values, own_inputs, their_inputs = frozen(
        info, own_half, sibling, grads, low, down_a, down_b, weight_a, weight_b, width, input_scale
    )
    got_values = plan.swap(values[tok_count:])
    value_output = (values[:tok_count] + got_values + own_values.astype(f32)).astype(bf16)
    input_gradient = merge(info, own_inputs, plan.swap(their_inputs), width)

    total_grad = jnp.concatenate([sum_a, sum_b, sum_up], axis=1)
    got_grad = plan.swap(total_grad[rank:])
    new_factors, new_first, new_second = adam(
        info, factors[0], first_moment[0], second_moment[0], total_grad[:rank], got_grad, width
    )
    return (value_output, input_gradient, new_factors[None], new_first[None], new_second[None])


def solution(mesh):
    placed = (
        P(("groups", "fsdp"), None),
        P(("groups", "fsdp"), None),
        P("fsdp", None),
        P(("groups", "fsdp")),
        P("groups"),
        P(("groups", "fsdp"), None, None),
        P(("groups", "fsdp"), None, None),
        P(("groups", "fsdp"), None, None),
    )
    return jax.shard_map(
        local,
        mesh=mesh,
        in_specs=placed,
        out_specs=(
            P(("groups", "fsdp"), None),
            P(("groups", "fsdp"), None),
            P(("groups", "fsdp"), None, None),
            P(("groups", "fsdp"), None, None),
            P(("groups", "fsdp"), None, None),
        ),
        check_vma=False,
    )
```

```python
import functools
import math

import jax
import jax.numpy as jnp
from jax import lax
from jax.experimental import pallas as pl
from jax.experimental.pallas import tpu as pltpu
from jax.sharding import PartitionSpec as P

adapter_scale = 0.25
beta_first = 0.9
beta_second = 0.95
adam_eps = 1e-08
learn_rate = 0.05
bias_first = 0.271
bias_second = 0.142625
contract_last = (((1,), (1,)), ((), ()))
contract_first = (((0,), (0,)), ((), ()))
f32 = jnp.float32
bf16 = jnp.bfloat16
vmem_bytes = 24 * 2**20


def dot(a, b, dims=(((1,), (0,)), ((), ()))):
    return lax.dot_general(a, b, dims, preferred_element_type=f32)


team = 4


class Plan:
    def __init__(self, devices):
        self.devices = devices
        self.teams = devices // team
        self.bits = self.teams.bit_length() - 1
        down = tuple(1 << i for i in reversed(range(self.bits)))
        self.orders = {"w": down, "d": down[-1:] + down[:-1]}

    def masks(self, stream):
        out = []
        for b in range(self.teams):
            m = 0
            for i, flip in enumerate(self.orders[stream]):
                if b >> i & 1:
                    m ^= flip
            out.append(m)
        return out

    def member(self, x, k):
        return lax.ppermute(x, "fsdp", [(i, i ^ k) for i in range(self.devices)])

    def step(self, x, stream, i):
        flip = self.orders[stream][i] * team
        return lax.ppermute(x, "fsdp", [(d, d ^ flip) for d in range(self.devices)])


def estimate(flops, bytes_accessed, transcendentals):
    return pl.CostEstimate(
        flops=flops // 1, bytes_accessed=bytes_accessed // 1, transcendentals=transcendentals
    )


def hbm(x):
    return pltpu.with_memory_space_constraint(x, pltpu.HBM)


whole_vmem = pl.BlockSpec(memory_space=pltpu.VMEM)
anywhere = pl.BlockSpec(memory_space=pl.ANY)


def params():
    return pltpu.CompilerParams(vmem_limit_bytes=vmem_bytes)


def join_kernel(count, late, *refs):
    refs = refs[: 2 * count] + refs[2 * count + late :]
    for i in range(count):
        own, got, out = refs[2 * i], refs[2 * i + 1], refs[2 * count + i]
        rows = own.shape[0]
        out[:rows] = own[...]
        out[rows:] = got[...]


def join(pairs, after=()):
    count = len(pairs)
    flat = [x for pair in pairs for x in pair]
    return pl.pallas_call(
        functools.partial(join_kernel, count, len(after)),
        in_specs=[whole_vmem] * (2 * count) + [anywhere] * len(after),
        out_specs=[whole_vmem] * count,
        out_shape=[jax.ShapeDtypeStruct((2 * x.shape[0], x.shape[1]), x.dtype) for x, _ in pairs],
        compiler_params=params(),
        cost_estimate=estimate(
            flops=0, bytes_accessed=4 * sum(x.size for x in flat), transcendentals=0
        ),
    )(*flat, *after)


def fold_kernel(count, late, *refs):
    refs = refs[: 2 * count] + refs[2 * count + late :]
    for i in range(count):
        keep, got = refs[2 * i], refs[2 * i + 1]
        kept, sent = refs[2 * count + 2 * i], refs[2 * count + 2 * i + 1]
        half = kept.shape[0]
        kept[...] = (keep[:half].astype(f32) + got[:half].astype(f32)).astype(kept.dtype)
        sent[...] = (keep[half:].astype(f32) + got[half:].astype(f32)).astype(sent.dtype)


def fold(pairs, after=()):
    count = len(pairs)
    flat = [x for pair in pairs for x in pair]
    shapes = [
        jax.ShapeDtypeStruct((x.shape[0] // 2, x.shape[1]), x.dtype) for x, _ in pairs for _ in "ks"
    ]
    out = pl.pallas_call(
        functools.partial(fold_kernel, count, len(after)),
        in_specs=[whole_vmem] * (2 * count) + [anywhere] * len(after),
        out_specs=[whole_vmem] * (2 * count),
        out_shape=shapes,
        compiler_params=params(),
        cost_estimate=estimate(
            flops=sum(x.size for x in flat),
            bytes_accessed=4 * sum(x.size for x in flat),
            transcendentals=0,
        ),
    )(*flat, *after)
    return [(out[2 * i], out[2 * i + 1]) for i in range(count)]


def tie_kernel(*refs):
    del refs


def tie(arrays, after):
    count = len(arrays)
    return pl.pallas_call(
        tie_kernel,
        in_specs=[anywhere] * (count + len(after)),
        out_specs=[anywhere] * count,
        out_shape=[jax.ShapeDtypeStruct(x.shape, x.dtype) for x in arrays],
        input_output_aliases={i: i for i in range(count)},
        cost_estimate=estimate(flops=0, bytes_accessed=0, transcendentals=0),
    )(*arrays, *after)


def members_of(info):
    j = info[0]
    return [j ^ k for k in range(team)]


def factor_kernel(width, wide, info, f_ref, *refs):
    quarter = wide // team
    for j, ref in zip(members_of(info), refs):
        for q in range(quarter // width):
            at = pl.multiple_of((team * q + j) * width, width)
            ref[:, q * width : (q + 1) * width] = f_ref[:, pl.ds(at, width)].astype(bf16)
        ref[:, quarter:] = f_ref[:, wide:].astype(bf16)


def split_factors(info, factors, width, wide):
    rank, total = factors.shape
    shape = jax.ShapeDtypeStruct((rank, wide // team + total - wide), bf16)
    return pl.pallas_call(
        functools.partial(factor_kernel, width, wide),
        in_specs=[pl.BlockSpec(memory_space=pltpu.SMEM), whole_vmem],
        out_specs=[whole_vmem] * team,
        out_shape=[shape] * team,
        cost_estimate=estimate(flops=0, bytes_accessed=1_000_000, transcendentals=0),
    )(info, factors)


def join_factors_kernel(quarter, *refs):
    up_ref, down_ref = refs[team:]
    rank = refs[0].shape[0]
    for k in range(team):
        down_ref[k * rank : (k + 1) * rank] = refs[k][:, :quarter]
        up_ref[k * rank : (k + 1) * rank] = refs[k][:, quarter:]


def join_factors(parts, quarter):
    rank, total = parts[0].shape
    return pl.pallas_call(
        functools.partial(join_factors_kernel, quarter),
        in_specs=[whole_vmem] * team,
        out_specs=[whole_vmem] * 2,
        out_shape=[
            jax.ShapeDtypeStruct((team * rank, total - quarter), bf16),
            jax.ShapeDtypeStruct((team * rank, quarter), bf16),
        ],
        cost_estimate=estimate(flops=0, bytes_accessed=16 * rank * total, transcendentals=0),
    )(*parts)


def deal_kernel(width, info, x_ref, t_ref, own_ref, *refs):
    quarter = own_ref.shape[1]
    for k, j in enumerate(members_of(info)):
        ref = refs[k - 1] if k else own_ref
        for q in range(quarter // width):
            at = pl.multiple_of((team * q + j) * width, width)
            ref[:, q * width : (q + 1) * width] = x_ref[:, pl.ds(at, width)]
        if k:
            ref[:, quarter:] = t_ref[...]


def deal(info, x, tail, width):
    rows, wide = x.shape
    step = rows // 6
    quarter = wide // team
    row = lambda n: pl.BlockSpec((step, n), lambda i, s: (i, 0))
    more = quarter + tail.shape[1]
    return pl.pallas_call(
        functools.partial(deal_kernel, width),
        grid_spec=pltpu.PrefetchScalarGridSpec(
            num_scalar_prefetch=1,
            grid=(6,),
            in_specs=[row(wide), row(tail.shape[1])],
            out_specs=[row(quarter)] + [row(more)] * (team - 1),
        ),
        out_shape=[jax.ShapeDtypeStruct((rows, quarter), bf16)]
        + [jax.ShapeDtypeStruct((rows, more), bf16)] * (team - 1),
        cost_estimate=estimate(flops=0, bytes_accessed=rows * wide * 4, transcendentals=0),
    )(info, x, tail)


def down_grad_kernel(half, scale, low_ref, low_two_ref, *refs):
    xs, (ka, sa, kb, sb) = refs[:team], refs[team:]
    q = pl.program_id(0)
    x = jnp.concatenate([ref[...] for ref in xs], axis=0)

    def one(low, keep, send):
        out = (scale * dot(low[...], x)).astype(bf16)
        cut = out.shape[0] // 2
        keep[...] = out[:cut]
        send[...] = out[cut:]

    @pl.when(q < half)
    def _():
        one(low_ref, ka, sa)

    @pl.when(q >= half)
    def _():
        one(low_two_ref, kb, sb)


def down_grads(low, low_two, xs, scale):
    rows, cols = xs[0].shape
    blocks = 4
    width = cols // blocks
    half = blocks // 2
    n = low.shape[0]
    whole = pl.BlockSpec(low.shape, lambda q: (0, 0))
    part = pl.BlockSpec((rows, width), lambda q: (0, q))
    first = pl.BlockSpec((n // 2, width), lambda q: (0, jnp.minimum(q, half - 1)))
    second = pl.BlockSpec((n // 2, width), lambda q: (0, jnp.maximum(q - half, 0)))
    out = pltpu.HBM((n // 2, cols // 2), bf16)
    return pl.pallas_call(
        functools.partial(down_grad_kernel, half, scale),
        grid=(blocks,),
        in_specs=[whole, whole] + [part] * team,
        out_specs=[first, first, second, second],
        out_shape=[out] * 4,
        compiler_params=params(),
        cost_estimate=estimate(
            flops=2 * team * rows * cols * n,
            bytes_accessed=2 * team * rows * cols + 2 * n * cols,
            transcendentals=0,
        ),
    )(low, low_two, *map(hbm, xs))


def project_kernel(rank, *refs):
    xs, (a_ref, owner_ref, target_ref, add_ref, o_ref, acc) = refs[:team], refs[team:]
    q = pl.program_id(0)

    @pl.when(q == 0)
    def _():
        acc[...] = jnp.zeros_like(acc)

    for k in range(team):
        acc[k] += dot(a_ref[...], xs[k][...], contract_last)

    @pl.when(q == pl.num_programs(0) - 1)
    def _():
        for k in range(team):
            kept = jnp.where(target_ref[k : k + 1] == owner_ref[...], acc[k], 0.0)
            at = slice(k * rank, (k + 1) * rank)
            out = add_ref[at]
            for i in range(kept.shape[0] // rank):
                out = out + kept[i * rank : (i + 1) * rank]
            o_ref[at] = out


def project(xs, down, owner, targets, add):
    rows, cols = xs[0].shape[0], down.shape[1]
    n = down.shape[0]
    width = cols // 4
    part = pl.BlockSpec((rows, width), lambda q: (0, q))
    still = lambda q: (0, 0)
    return pl.pallas_call(
        functools.partial(project_kernel, add.shape[0] // team),
        grid=(4,),
        in_specs=[part] * team
        + [
            pl.BlockSpec((n, width), lambda q: (0, q)),
            pl.BlockSpec((n, 1), still),
            pl.BlockSpec((team, rows), still),
            pl.BlockSpec(add.shape, still),
        ],
        out_specs=pl.BlockSpec(add.shape, still),
        out_shape=jax.ShapeDtypeStruct(add.shape, f32),
        scratch_shapes=[pltpu.VMEM((team, n, rows), f32)],
        compiler_params=params(),
        cost_estimate=estimate(
            flops=2 * team * rows * cols * n,
            bytes_accessed=2 * (team * rows + n) * cols,
            transcendentals=0,
        ),
    )(*map(hbm, (*xs, down, owner, targets, add)))


def lora_kernel(scale, *refs):
    parts, (owner_ref, target_ref, g_ref, up_ref, keep_ref, send_ref, v_ref) = refs[:team], refs[team:]
    rank = parts[0].shape[0] // team
    rows = parts[0].shape[1]
    count = owner_ref.shape[0]
    grad = None
    for m in range(team):
        total = None
        for k in range(team):
            one = parts[k][(m ^ k) * rank : ((m ^ k) + 1) * rank]
            total = one if total is None else total + one
        rounded = (scale * total).astype(bf16).astype(f32)
        many = jnp.concatenate([rounded] * (count // rank), axis=0)
        own = jnp.where(target_ref[m : m + 1] == owner_ref[...], many, 0.0).astype(bf16)
        more = dot(own, g_ref[m * rows : (m + 1) * rows])
        grad = more if grad is None else grad + more
        if m == 0:
            v_ref[...] = adapter_scale * dot(own, up_ref[...], contract_first)
    cut = count // 2
    keep_ref[...] = adapter_scale * grad[:cut]
    send_ref[...] = adapter_scale * grad[cut:]


def lora(parts, owner, targets, grads, up, scale):
    rows = parts[0].shape[1]
    half = jax.ShapeDtypeStruct((up.shape[0] // 2, grads.shape[1]), f32)
    return pl.pallas_call(
        functools.partial(lora_kernel, scale),
        in_specs=[whole_vmem] * (team + 4),
        out_specs=[whole_vmem] * 3,
        out_shape=[half, half, jax.ShapeDtypeStruct((rows, up.shape[1]), f32)],
        compiler_params=params(),
        cost_estimate=estimate(
            flops=2 * rows * up.size, bytes_accessed=2_000_000, transcendentals=0
        ),
    )(*parts, owner, targets, grads, up)


def frozen_kernel(half, width, scale, info, *refs):
    x0, x1, y0, y1, a0, a1, b0, b1, u_ref, w_ref, g_ref, low_ref, o_ref, t_ref, v_ref, acc = refs
    b = pl.program_id(0)

    @pl.when(b == 0)
    def _():
        acc[...] = jnp.zeros_like(acc)

    n = x0.shape[0]
    cut = a0.shape[0]
    acc[:n] += dot(x0[...], u_ref[...]) + dot(x1[...], w_ref[...])
    acc[n:] += dot(y0[...], u_ref[...]) + dot(y1[...], w_ref[...])
    for part, one, two, rows in ((0, a0, b0, u_ref), (half, a1, b1, w_ref)):
        lora = scale * (dot(low_ref[:, :cut], one[...]) + dot(low_ref[:, cut:], two[...]))
        out = dot(g_ref[...], rows[...], contract_last) + lora.astype(bf16).astype(f32)
        out = out.astype(bf16)
        at = pl.ds(pl.multiple_of(info[1 + part + b] * width, width), width)
        o_ref[:, at] = out[:n]
        t_ref[:, at] = out[n:]

    @pl.when(b == pl.num_programs(0) - 1)
    def _():
        quarter = o_ref.shape[1] - acc.shape[1]
        o_ref[:, quarter:] = acc[:n].astype(bf16)
        t_ref[:, quarter:] = acc[n:].astype(bf16)
        v_ref[...] = acc[:n]


def frozen(info, x, y, grads, low, downs, weights, width, scale, at):
    rows, kv = x.shape[0], grads.shape[1]
    n, cols = downs[0].shape
    half = cols // width // 2
    pair = lambda b, s: (at, 0)
    still = lambda b, s: (0, 0)
    early = lambda b, s: (0, s[1 + b])
    late = lambda b, s: (0, s[1 + half + b])
    out = pltpu.HBM((rows, cols + kv), bf16)
    return pl.pallas_call(
        functools.partial(frozen_kernel, half, width, scale),
        grid_spec=pltpu.PrefetchScalarGridSpec(
            num_scalar_prefetch=1,
            grid=(half,),
            in_specs=[pl.BlockSpec((rows, width), early), pl.BlockSpec((rows, width), late)] * 2
            + [pl.BlockSpec((n, width), early), pl.BlockSpec((n, width), late)] * 2
            + [pl.BlockSpec((width, kv), lambda b, s: (b, 0))] * 2
            + [pl.BlockSpec((2 * rows, kv), pair), pl.BlockSpec((2 * rows, 2 * n), pair)],
            out_specs=[pl.BlockSpec((rows, cols + kv), still)] * 2 + [pl.BlockSpec((rows, kv), still)],
            scratch_shapes=[pltpu.VMEM((2 * rows, kv), f32)],
        ),
        out_shape=[out, out, pltpu.HBM((rows, kv), f32)],
        compiler_params=params(),
        cost_estimate=estimate(
            flops=8 * rows * cols * (n + kv),
            bytes_accessed=(8 * rows + 4 * n + 2 * kv) * cols,
            transcendentals=0,
        ),
    )(info, *map(hbm, (x, x, y, y, downs[0], downs[0], downs[1], downs[1], *weights, grads, low)))


def merge_kernel(width, quarter, info, *refs):
    o_ref = refs[team]
    for j, ref in zip(members_of(info), refs):
        for q in range(quarter // width):
            at = pl.multiple_of((team * q + j) * width, width)
            o_ref[:, pl.ds(at, width)] = ref[:, q * width : (q + 1) * width]


def merge(info, parts, width, quarter):
    rows, cols = parts[0].shape
    step = rows // 6
    small = pl.BlockSpec((step, cols), lambda i, s: (i, 0))
    return pl.pallas_call(
        functools.partial(merge_kernel, width, quarter),
        grid_spec=pltpu.PrefetchScalarGridSpec(
            num_scalar_prefetch=1,
            grid=(6,),
            in_specs=[small] * team,
            out_specs=pl.BlockSpec((step, team * quarter), lambda i, s: (i, 0)),
        ),
        out_shape=jax.ShapeDtypeStruct((rows, team * quarter), bf16),
        cost_estimate=estimate(flops=0, bytes_accessed=16 * rows * cols, transcendentals=0),
    )(info, *map(hbm, parts))


def adam_kernel(width, wide, info, f_ref, m_ref, v_ref, *refs):
    grads, (nf_ref, nm_ref, nv_ref) = refs[:team], refs[team:]
    quarter = wide // team
    tail = (f_ref.shape[1] - wide) // team

    def update(at, g):
        first = beta_first * m_ref[:, at] + (1.0 - beta_first) * g
        second = beta_second * v_ref[:, at] + (1.0 - beta_second) * g * g
        step = first / bias_first / (jnp.sqrt(second / bias_second) + adam_eps)
        nf_ref[:, at] = f_ref[:, at] - learn_rate * step
        nm_ref[:, at] = first
        nv_ref[:, at] = second

    for j, ref in zip(members_of(info), grads):
        for q in range(quarter // width):
            at = pl.multiple_of((team * q + j) * width, width)
            update(pl.ds(at, width), ref[:, q * width : (q + 1) * width].astype(f32))
        update(pl.ds(pl.multiple_of(wide + j * tail, tail), tail), ref[:, quarter:].astype(f32))


def adam(info, factors, first, second, grads, width, wide):
    shape = jax.ShapeDtypeStruct(factors.shape, f32)
    return pl.pallas_call(
        functools.partial(adam_kernel, width, wide),
        in_specs=[pl.BlockSpec(memory_space=pltpu.SMEM)] + [whole_vmem] * (3 + team),
        out_specs=[whole_vmem] * 3,
        out_shape=[shape] * 3,
        compiler_params=params(),
        cost_estimate=estimate(
            flops=20 * factors.size, bytes_accessed=32 * factors.size, transcendentals=0
        ),
    )(info, factors, first, second, *grads)


def local(
    tokens, out_grad, base_weight, adapter_ids, adapter_home, factors, first_moment, second_moment
):
    tok_count, wide = tokens.shape
    value_width = out_grad.shape[1]
    rank = factors.shape[1]
    width = base_weight.shape[0]
    plan = Plan(lax.axis_size("fsdp"))
    bits = plan.bits
    quarter = wide // team
    input_scale = 1.0 / math.sqrt(wide)
    me = lax.axis_index("fsdp").astype(jnp.int32)
    group, member = me // team, me % team
    mask_d = jnp.array(plan.masks("d"), jnp.int32)
    mask_w = jnp.array(plan.masks("w"), jnp.int32)
    info = jnp.concatenate([member[None], group ^ mask_w])

    weight = base_weight
    got_weight = plan.step(weight, "w", 0)
    parts = split_factors(info, factors[0], width, wide)
    got_parts = [plan.member(parts[k], k) for k in range(1, team)]

    columns = jnp.arange(plan.devices, dtype=jnp.int32)
    adapter_hot = (adapter_ids[:, None] == columns[None, :]).astype(jnp.int32)
    target = jnp.sum(adapter_hot * adapter_home[None, :], axis=1)
    tail = jnp.concatenate(
        [out_grad, jnp.broadcast_to(target[:, None], (tok_count, 128)).astype(bf16)], axis=1
    )
    dealt = deal(info, tokens, tail, width)
    got = [plan.member(dealt[k], k) for k in range(1, team)]
    xs = [dealt[0]] + got
    tails = jnp.concatenate([tail] + [x[:, quarter:] for x in got], axis=0)
    grads = tails[:, :value_width]
    targets = tails[:, value_width].astype(jnp.int32)
    target_rows = targets.reshape(team, tok_count)

    up, down = join_factors([parts[0]] + got_parts, quarter)
    (weight,) = join(((weight, got_weight),))
    up, down = join(((up, plan.step(up, "d", 0)), (down, plan.step(down, "d", 0))), (weight,))
    for i in range(1, bits - 1):
        (up,) = join(((up, plan.step(up, "d", i)),))
    (up_all,) = join(((up, plan.step(up, "d", bits - 1)),))
    for i in range(1, bits - 1):
        (weight,) = join(((weight, plan.step(weight, "w", i)),))
        (down,) = join(((down, plan.step(down, "d", i)),), (weight,))
    weights = (weight, plan.step(weight, "w", bits - 1))
    downs = (down, plan.step(down, "d", bits - 1))

    within = jnp.arange(team * rank, dtype=jnp.int32) // rank

    def owner_of(mask):
        return (team * (group ^ mask)[:, None] + (member ^ within)[None, :]).reshape(-1)

    owner = owner_of(mask_d)
    owner_two = owner_of(mask_w)
    places = jnp.array([plan.masks("d").index(m) for m in plan.masks("w")], jnp.int32)
    up_two = up_all.reshape(plan.teams, team * rank, value_width)[places].reshape(up_all.shape)

    def low_of(up, owner):
        out = adapter_scale * dot(up, grads, contract_last)
        return jnp.where(owner[:, None] == targets[None, :], out, 0.0).astype(bf16)

    low = adapter_scale * dot(grads, up_all, contract_last)
    low = jnp.where(targets[:, None] == owner[None, :], low, 0.0).astype(bf16)
    keep_a, send_a, keep_b, send_b = down_grads(
        low_of(up_all, owner), low_of(up_two, owner_two), xs, input_scale
    )
    n = down.shape[0]
    nothing = jnp.zeros((team * rank, tok_count), f32)
    part = project(xs, downs[0], owner[:n, None], target_rows, nothing)

    (info_far,) = tie((info,), (keep_a, part))
    send_a, send_b = tie((send_a, send_b), (weights[1], downs[1]))
    far = frozen(info_far, xs[2], xs[3], grads, low, downs, weights, width, input_scale, 1)
    (part,) = tie((part,), (far[2],))
    from_far = [plan.member(far[0], 2), plan.member(far[1], 3)]
    part = project(xs, downs[1], owner[n:, None], target_rows, part)
    near = frozen(info_far, xs[0], xs[1], grads, low, downs, weights, width, input_scale, 0)
    done = [near[0], plan.member(near[1], 1)] + from_far

    value_part = value_width // team
    part_grads = lax.dynamic_slice_in_dim(grads, member * value_part, value_part, 1)
    keep_up, send_up, own_values = lora(
        [part] + [plan.member(part, k) for k in range(1, team)],
        owner[:, None],
        target_rows,
        part_grads,
        up_all,
        input_scale,
    )
    got_up = plan.step(send_up, "d", bits - 1)
    first_up = got_up
    lora_up = keep_up
    for i in reversed(range(bits)):
        if i < bits - 1:
            got_up = plan.step(send_up, "d", i)
        if i > 0:
            ((keep_up, send_up),) = fold(((keep_up, got_up),))
    sum_up = keep_up + got_up

    for i in reversed(range(bits)):
        got_a = plan.step(send_a, "d", i)
        got_b = plan.step(send_b, "w", i)
        if i > 0:
            (keep_a, send_a), (keep_b, send_b) = fold(
                ((keep_a, got_a), (keep_b, got_b)), (first_up,) if i == bits - 1 else ()
            )
    sum_a = keep_a.astype(f32) + got_a.astype(f32)
    sum_b = keep_b.astype(f32) + got_b.astype(f32)

    sums = jnp.concatenate([sum_a, sum_b, sum_up], axis=1)
    mine = [sums[:rank]]
    for k in range(1, team):
        mine.append(plan.member(sums[k * rank : (k + 1) * rank].astype(bf16), k))
    new_factors, new_first, new_second = adam(
        info, factors[0], first_moment[0], second_moment[0], mine, width, wide
    )

    values = near[2]
    for x in done[1:]:
        values = values + x[:, quarter:].astype(f32)
    value_output = (values + own_values.astype(bf16).astype(f32)).astype(bf16)
    input_gradient = merge(info, done, width, quarter)
    return (value_output, input_gradient, new_factors[None], new_first[None], new_second[None])


def solution(mesh):
    placed = (
        P(("groups", "fsdp"), None),
        P(("groups", "fsdp"), None),
        P("fsdp", None),
        P(("groups", "fsdp")),
        P("groups"),
        P(("groups", "fsdp"), None, None),
        P(("groups", "fsdp"), None, None),
        P(("groups", "fsdp"), None, None),
    )
    return jax.shard_map(
        local,
        mesh=mesh,
        in_specs=placed,
        out_specs=(
            P(("groups", "fsdp"), None),
            P(("groups", "fsdp"), None),
            P(("groups", "fsdp"), None, None),
            P(("groups", "fsdp"), None, None),
            P(("groups", "fsdp"), None, None),
        ),
        check_vma=False,
    )
```
